512 devices in a mesh: ctx: 128 (over z_hi, y, x), ch: 4 (over z_lo, core).
Axes of the slice: x: 4, y: 8, z: 8 (z_hi: 4, z_lo: 2; z = z_hi * 2 + z_lo), core: 2. Of those that a mesh axis runs over, the one named last changes fastest.
Arguments:
- gate_in: bfloat16 [16384, 4096], P('ctx', 'ch'), may hold values from -6 to 6
- values: bfloat16 [16384, 4096], P('ctx', 'ch'), may hold values from -6 to 6
- filters: float32 [16384, 1024], P('ctx'), may hold values from -0.046875 to 0.046875
- out_grad: bfloat16 [16384, 4096], P('ctx', 'ch'), may hold values from -6 to 6
Outputs:
- gate_grad: float32 [16384, 4096], P('ctx', 'ch')
- value_grad: float32 [16384, 4096], P('ctx', 'ch')
- filter_grad: float32 [16384, 1024], P('ctx', 'ch')
The draws below stay inside these ranges and needn't reach their ends.
All inputs are finite; a program needn't handle non-finite values.
Results may differ from the reference program's by a relative error of at most 0.0029.
Values sent between devices are 32-bit elements; how exact they have to be, the bound alone decides.
A program may use at most 64 MiB of HBM per device.

```python
import math
import jax
import jax.numpy as jnp
from jax import lax

C = 4096
SEQ = 16384
FILT = 1024


def block_levels(rng, extent, pieces, least, high):
    level, own = 1.0, jax.random.fold_in(rng, 6)
    for position, parts in pieces:
        heights = jnp.exp(jax.random.uniform(jax.random.fold_in(own, position), (parts,), jnp.float32, least / len(pieces), high / len(pieces)))
        level = level * jnp.repeat(heights, extent[position] // parts).reshape([-1 if axis == position else 1 for axis in range(len(extent))])
    return level


def normal_values(rng, extent, spread, bound, pieces=(), dtype=jnp.bfloat16):
    values = jax.random.normal(rng, extent, jnp.float32) * spread
    if len(pieces) > 0:
        values = block_levels(rng, extent, pieces, -0.22, 0.18) * values
    return jnp.clip(values, min=-bound, max=bound).astype(dtype)


def setup_inputs(seed: int = 0) -> dict:
    keys = jax.random.split(jax.random.key(seed), 5)
    gate_in = normal_values(keys[0], (SEQ, C), 1.0, 6.0, ((0, 128), (1, 4)))
    values = normal_values(keys[1], (SEQ, C), 1.0, 6.0, ((0, 128), (1, 4)))
    filters = normal_values(keys[2], (SEQ, FILT), SEQ ** -0.5, 0.046875, ((0, 128),), jnp.float32)
    out_grad = normal_values(keys[3], (SEQ, C), 1.0, 6.0, ((0, 128), (1, 4)))
    return dict(gate_in=gate_in, values=values, filters=filters, out_grad=out_grad)


def reference(gate_in, values, filters, out_grad):
    share = C // FILT
    block_width = min(FILT, 128)
    block_count = FILT // block_width
    length = 2 * SEQ
    factor = 1.0 / math.sqrt(share * SEQ)

    def split_blocks(array):
        return array.reshape(SEQ, share, block_count, block_width).transpose(2, 0, 1, 3)
    inner_low = (out_grad.astype(jnp.float32) * gate_in.astype(jnp.float32)).astype(jnp.bfloat16)
    inner_low = lax.optimization_barrier(inner_low)

    def one_block(items):
        grad_block, value_block, inner_block, filter_block = items
        value_spec = jnp.fft.rfft(value_block.astype(jnp.float32), n=length, axis=0)
        inner_spec = jnp.fft.rfft(inner_block.astype(jnp.float32), n=length, axis=0)
        filter_spec = jnp.fft.rfft(filter_block, n=length, axis=0)[:, None, :]
        conv_out = jnp.fft.irfft(filter_spec * value_spec, n=length, axis=0)[:SEQ]
        value_grad = jnp.fft.irfft(jnp.conj(filter_spec) * inner_spec, n=length, axis=0)[:SEQ]
        summed = lax.optimization_barrier(jnp.sum(jnp.conj(value_spec) * inner_spec, axis=1))
        filter_grad = jnp.fft.irfft(summed, n=length, axis=0)[:SEQ]
        return (grad_block.astype(jnp.float32) * conv_out, value_grad, filter_grad * factor)
    filter_blocks = filters.reshape(SEQ, block_count, block_width).transpose(1, 0, 2)
    gate_grad, value_grad, filter_grad = lax.map(one_block, (split_blocks(out_grad), split_blocks(values), split_blocks(inner_low), filter_blocks))
    gate_grad = gate_grad.transpose(1, 2, 0, 3).reshape(SEQ, C)
    value_grad = value_grad.transpose(1, 2, 0, 3).reshape(SEQ, C)
    filter_grad = filter_grad.transpose(1, 0, 2).reshape(SEQ, FILT)
    return (gate_grad, value_grad, filter_grad)
```

```python
import functools

import jax
import jax.numpy as jnp
from jax import lax
from jax.experimental import pallas as pl
from jax.experimental.pallas import tpu as pltpu
from jax.sharding import PartitionSpec as P

BF = jnp.bfloat16
F32 = jnp.float32
MESH = pl.DeviceIdType.MESH
VM = pl.BlockSpec(memory_space=pltpu.VMEM)


def dot(a, b, ca=1, cb=0):
    return lax.dot_general(a, b, (((ca,), (cb,)), ((), ())), preferred_element_type=F32)


def coords():
    ctx = lax.axis_index("ctx")
    ch = lax.axis_index("ch")
    return ctx % 4, (ctx // 4) % 8, (ctx // 32) * 2 + ch // 2, ch % 2


def peer(x, y, z, c):
    return (z // 2) * 32 + y * 4 + x, (z % 2) * 2 + c


def place(ctx, ch):
    return (ctx % 2) * 256 + (ctx // 2) * 4 + ch


def pack_kernel(gate_ref, values_ref, filters_ref, grad_ref, x_ref, f_ref, wide):
    inner = (grad_ref[...].astype(F32) * gate_ref[...].astype(F32)).astype(BF)
    for s, signal in enumerate((values_ref[...], inner)):
        wide[...] = signal.astype(F32).T
        for p in range(2):
            x_ref[pl.ds(2 * s + p, 512, stride=4), :] = wide[pl.ds(p, 512, stride=2), :]
    start = pl.multiple_of(lax.axis_index("ch") * 256, 256)
    f_ref[...] = filters_ref[:, pl.ds(start, 256)].T


def gather_kernel(x_ref, f_ref, ox_ref, of_ref, lx, lf, sx, rx, sf, rf):
    x, y, z, c = coords()
    ctx, ch = peer(x, y, z, c)
    row = place(ctx, ch)
    own_x = pltpu.make_async_copy(x_ref.at[ch * 128 + ctx], ox_ref.at[row], lx)
    own_f = pltpu.make_async_copy(f_ref.at[ctx], of_ref.at[ctx], lf)
    own_x.start()
    own_f.start()

    def body(i, _):
        x2 = (x + i // 128) % 4
        y2 = (y + i // 2) % 8
        z2 = (z + i // 16) % 8
        c2 = (c + i) % 2
        ctx2, ch2 = peer(x2, y2, z2, c2)
        pltpu.make_async_remote_copy(
            x_ref.at[ch2 * 128 + ctx2], ox_ref.at[row], sx, rx, device_id=(ctx2, ch2), device_id_type=MESH
        ).start()
        return 0

    lax.fori_loop(1, 512, body, 0)

    def body_f(i, _):
        ctx2 = (ctx + i) % 128
        pltpu.make_async_remote_copy(
            f_ref.at[ctx2], of_ref.at[ctx], sf, rf, device_id=(ctx2, ch), device_id_type=MESH
        ).start()
        return 0

    lax.fori_loop(1, 128, body_f, 0)
    own_x.wait()
    own_f.wait()
    for sem in (sx, rx):
        pltpu.make_async_copy(x_ref.at[pl.ds(0, 511)], ox_ref.at[pl.ds(0, 511)], sem).wait()
    for sem in (sf, rf):
        pltpu.make_async_copy(f_ref.at[pl.ds(0, 127)], of_ref.at[pl.ds(0, 127)], sem).wait()


def scatter_kernel(x_ref, f_ref, ox_ref, of_ref, lx, lf, sx, rx, sf, rf):
    x, y, z, c = coords()
    ctx, ch = peer(x, y, z, c)
    hub = ch * 128 + ctx
    own_x = pltpu.make_async_copy(x_ref.at[place(ctx, ch)], ox_ref.at[hub], lx)
    own_f = pltpu.make_async_copy(f_ref.at[ctx], of_ref.at[ctx], lf)
    own_x.start()
    own_f.start()

    def body(i, _):
        x2 = (x + i // 128) % 4
        y2 = (y + i // 2) % 8
        z2 = (z + i // 16) % 8
        c2 = (c + i) % 2
        ctx2, ch2 = peer(x2, y2, z2, c2)
        pltpu.make_async_remote_copy(
            x_ref.at[place(ctx2, ch2)], ox_ref.at[hub], sx, rx, device_id=(ctx2, ch2), device_id_type=MESH
        ).start()
        return 0

    lax.fori_loop(1, 512, body, 0)

    def body_f(i, _):
        ctx2 = (ctx + i) % 128
        pltpu.make_async_remote_copy(
            f_ref.at[ctx2], of_ref.at[ctx], sf, rf, device_id=(ctx2, ch), device_id_type=MESH
        ).start()
        return 0

    lax.fori_loop(1, 128, body_f, 0)
    own_x.wait()
    own_f.wait()
    for sem in (sx, rx):
        pltpu.make_async_copy(x_ref.at[pl.ds(0, 511)], ox_ref.at[pl.ds(0, 511)], sem).wait()
    for sem in (sf, rf):
        pltpu.make_async_copy(f_ref.at[pl.ds(0, 127)], of_ref.at[pl.ds(0, 127)], sem).wait()


def exchange(body, x, f, name):
    shapes = (jax.ShapeDtypeStruct((512, 4, 128), F32), jax.ShapeDtypeStruct((128, 2, 128), F32))
    ox, of = pl.pallas_call(
        body,
        out_shape=shapes,
        in_specs=[VM, VM],
        out_specs=(VM, VM),
        scratch_shapes=[pltpu.SemaphoreType.DMA] * 6,
        name=name,
        compiler_params=pltpu.CompilerParams(has_side_effects=True),
    )(x.reshape(512, 4, 128), f.reshape(128, 2, 128))
    return ox.reshape(2048, 128), of.reshape(256, 128)


def hub_kernel(r_ref, f_ref, o_ref, of_ref, pad, xl, il, ifw, y_acc, v_acc, phi, plo):
    ri = lax.broadcasted_iota(jnp.int32, (256, 256), 0)
    ci = lax.broadcasted_iota(jnp.int32, (256, 256), 1)
    flip = (ri + ci == 255).astype(F32).astype(BF)
    keep = lax.broadcasted_iota(jnp.int32, (128, 128), 1) >= lax.broadcasted_iota(jnp.int32, (128, 128), 0)
    early = lax.broadcasted_iota(jnp.int32, (128, 128), 1) <= lax.broadcasted_iota(jnp.int32, (128, 128), 0)
    lane_rev = 127 - lax.broadcasted_iota(jnp.int32, (256, 128), 1)
    for p in range(2):
        def load(s):
            return jnp.concatenate([r_ref[pl.ds(1024 * h + 2 * s + p, 256, stride=4), :] for h in range(2)], axis=1)
        x = load(0)
        g = load(1)
        g_low = g.astype(BF)
        g_rev = dot(g_low, flip)
        v_rev = dot(flip, x.astype(BF), 1, 1).astype(BF)
        pad[0:16, :] = jnp.zeros((16, 256), F32)
        pad[272:288, :] = jnp.zeros((16, 256), F32)
        pad[16:272, :] = x
        for m0 in range(4):
            sh = pad[16 - 4 * m0:272 - 4 * m0, :].astype(BF)
            xl[:, 256 * m0:256 * m0 + 128] = sh[:, 128:256]
            xl[:, 256 * m0 + 128:256 * m0 + 256] = sh[:, 0:128]
        pad[16:272, :] = g_rev
        for m0 in range(4):
            sh = pad[16 + 4 * m0:272 + 4 * m0, :].astype(BF)
            il[:, 256 * m0:256 * m0 + 128] = sh[:, 128:256]
            il[:, 256 * m0 + 128:256 * m0 + 256] = sh[:, 0:128]
        pad[16:272, :] = g
        for m0 in range(4):
            ifw[:, 256 * m0:256 * m0 + 256] = pad[16 + 4 * m0:272 + 4 * m0, :].astype(BF)
        phi[:, 0:128] = jnp.zeros((128, 128), BF)
        plo[:, 0:128] = jnp.zeros((128, 128), BF)
        prev = jnp.zeros((128, 128), F32)
        for u in range(128):
            row = jnp.broadcast_to(f_ref[pl.ds(2 * u + p, 1), :], (128, 128))
            turned = pltpu.roll(row, 0, 1, stride=1, stride_axis=0)
            band = jnp.where(keep, turned, prev)
            high = band.astype(BF)
            phi[:, 128 * (u + 1):128 * (u + 2)] = high
            plo[:, 128 * (u + 1):128 * (u + 2)] = (band - high.astype(F32)).astype(BF)
            prev = turned
        y_acc[...] = jnp.zeros((256, 256), F32)
        v_acc[...] = jnp.zeros((256, 256), F32)
        carry = jnp.zeros((128, 128), F32)
        before = jnp.zeros((128, 128), F32)
        for m1 in range(16):
            n = 256 - 16 * m1
            lhs = jnp.concatenate([xl[0:n, :], il[16 * m1:256, :]], axis=0)
            def slabs(ref):
                return jnp.concatenate([ref[:, 128 * k + 1024 * m1:128 * k + 1024 * m1 + 256] for k in range(8)], axis=0)
            res = dot(lhs, slabs(phi)) + dot(lhs, slabs(plo))
            y_acc[16 * m1:256, :] += res[0:n]
            v_acc[0:n, :] += res[n:]
            kk = n if n % 128 == 0 else (256 if n > 128 else 128)
            rhs = ifw[16 * m1:256, :]
            if kk > n:
                rhs = jnp.concatenate([rhs, jnp.zeros((kk - n, 1024), BF)], axis=0)
            z = dot(v_rev[:, 0:kk], rhs)
            for t in range(8):
                w = z[0:128, 128 * t:128 * t + 128]
                w = w + (carry if t == 0 else z[128:256, 128 * t - 128:128 * t])
                turned = pltpu.roll(w, 1, 1, stride=1, stride_axis=0)
                if 8 * m1 + t >= 2:
                    u = 8 * m1 + t - 2
                    of_ref[pl.ds(2 * u + p, 1), :] = jnp.sum(jnp.where(early, before, turned), axis=0, keepdims=True) * (1.0 / 256.0)
                before = turned
            carry = z[128:256, 896:1024]
        turned = pltpu.roll(carry, 1, 1, stride=1, stride_axis=0)
        of_ref[pl.ds(2 * 126 + p, 1), :] = jnp.sum(jnp.where(early, before, turned), axis=0, keepdims=True) * (1.0 / 256.0)
        of_ref[pl.ds(2 * 127 + p, 1), :] = jnp.sum(jnp.where(early, turned, 0.0), axis=0, keepdims=True) * (1.0 / 256.0)
        for h in range(2):
            o_ref[pl.ds(1024 * h + p, 256, stride=4), :] = y_acc[:, 128 * h:128 * h + 128]
            back = v_acc[:, 128 * (1 - h):128 * (1 - h) + 128]
            o_ref[pl.ds(1024 * h + 2 + p, 256, stride=4), :] = jnp.take_along_axis(back, lane_rev, axis=1)

def hub(r, f):
    vm = pl.BlockSpec(memory_space=pltpu.VMEM)
    return pl.pallas_call(hub_kernel,
        out_shape=(jax.ShapeDtypeStruct((2048, 128), F32), jax.ShapeDtypeStruct((256, 128), F32)),
        in_specs=[vm, vm], out_specs=(vm, vm), name="hub",
        scratch_shapes=[pltpu.VMEM((288, 256), F32), pltpu.VMEM((256, 1024), BF), pltpu.VMEM((256, 1024), BF), pltpu.VMEM((256, 1024), BF),
                        pltpu.VMEM((256, 256), F32), pltpu.VMEM((256, 256), F32), pltpu.VMEM((128, 16512), BF), pltpu.VMEM((128, 16512), BF)],
        compiler_params=pltpu.CompilerParams(vmem_limit_bytes=48 * 1024 * 1024))(r, f)

def unpack_kernel(b_ref, f_ref, grad_ref, gate_grad_ref, value_grad_ref, filter_grad_ref, wide):
    for p in range(2):
        wide[pl.ds(p, 512, stride=2), :] = b_ref[pl.ds(p, 512, stride=4), :]
    gate_grad_ref[...] = wide[...].T * grad_ref[...].astype(F32)
    for p in range(2):
        wide[pl.ds(p, 512, stride=2), :] = b_ref[pl.ds(2 + p, 512, stride=4), :]
    value_grad_ref[...] = wide[...].T
    filter_grad_ref[...] = f_ref[...].T


def per_device(gate_in, values, filters, out_grad):
    x, f = pl.pallas_call(
        pack_kernel,
        out_shape=(jax.ShapeDtypeStruct((2048, 128), F32), jax.ShapeDtypeStruct((256, 128), F32)),
        in_specs=[VM] * 4,
        out_specs=(VM, VM),
        scratch_shapes=[pltpu.VMEM((1024, 128), F32)],
        name="pack",
    )(gate_in, values, filters, out_grad)
    x, f = exchange(gather_kernel, x, f, "to_hubs")
    x, f = hub(x, f)
    x, f = exchange(scatter_kernel, x, f, "from_hubs")
    return pl.pallas_call(
        unpack_kernel,
        out_shape=(
            jax.ShapeDtypeStruct((128, 1024), F32),
            jax.ShapeDtypeStruct((128, 1024), F32),
            jax.ShapeDtypeStruct((128, 256), F32),
        ),
        in_specs=[VM] * 3,
        out_specs=(VM,) * 3,
        scratch_shapes=[pltpu.VMEM((1024, 128), F32)],
        name="unpack",
    )(x, f, out_grad)


def solution(mesh):
    return jax.shard_map(
        per_device,
        mesh=mesh,
        in_specs=(P("ctx", "ch"), P("ctx", "ch"), P("ctx", None), P("ctx", "ch")),
        out_specs=(P("ctx", "ch"), P("ctx", "ch"), P("ctx", "ch")),
        check_vma=False,
    )
```

```python
import functools

import jax
import jax.numpy as jnp
from jax import lax
from jax.experimental import pallas as pl
from jax.experimental.pallas import tpu as pltpu
from jax.sharding import PartitionSpec as P

BF = jnp.bfloat16
F32 = jnp.float32
MESH = pl.DeviceIdType.MESH
VM = pl.BlockSpec(memory_space=pltpu.VMEM)


def dot(a, b, ca=1, cb=0):
    return lax.dot_general(a, b, (((ca,), (cb,)), ((), ())), preferred_element_type=F32)


def flatten(x, y, zh, zl):
    ctx = zh * 32 + y * 4 + x
    return zl * 128 + ctx, lax.rem(ctx, 2) * 128 + lax.div(ctx, 2) * 2 + zl, ctx


def every_chip(visit):
    ctx = lax.axis_index("ctx")
    ch = lax.axis_index("ch")
    core = lax.rem(ch, 2)
    x = lax.rem(ctx, 4)
    y = lax.rem(lax.div(ctx, 4), 8)
    z = lax.div(ctx, 32) * 2 + lax.div(ch, 2)
    ys = [lax.rem(y + d, 8) for d in range(8)]

    def body(i, _):
        z2 = lax.rem(z + i, 8)
        x2 = lax.rem(x + lax.div(i, 8), 4)
        zh, zl = lax.div(z2, 2), lax.rem(z2, 2)
        for d in range(8):
            def one(y2=ys[d]):
                hub, place, ctx2 = flatten(x2, y2, zh, zl)
                visit(hub, place, ctx2, zl * 2 + core)
            if d == 0:
                pl.when(i > 0)(one)
            else:
                one()
        return 0

    lax.fori_loop(0, 32, body, 0)


def every_row(visit):
    ctx = lax.axis_index("ctx")

    def body(i, _):
        for k in range(8):
            def one(d=8 * i + k):
                visit(lax.rem(ctx + d, 128))
            if k == 0:
                pl.when(i > 0)(one)
            else:
                one()
        return 0

    lax.fori_loop(0, 16, body, 0)


def products(p, r_ref, f_ref, o_ref, of_ref, pad, xl, il, ifw, y_acc, v_acc, phi, plo):
    ri = lax.broadcasted_iota(jnp.int32, (256, 256), 0)
    ci = lax.broadcasted_iota(jnp.int32, (256, 256), 1)
    flip = (ri + ci == 255).astype(F32).astype(BF)
    row128 = lax.broadcasted_iota(jnp.int32, (128, 128), 0)
    lane128 = lax.broadcasted_iota(jnp.int32, (128, 128), 1)
    keep = lane128 >= row128
    early = lane128 <= row128
    lane_rev = 127 - lax.broadcasted_iota(jnp.int32, (256, 128), 1)

    def load(s):
        return jnp.concatenate(
            [r_ref[pl.ds(1024 * p + 512 * h + s, 256, stride=2), :] for h in range(2)], axis=1
        )

    x = load(0)
    g = load(1)
    g_rev = dot(g.astype(BF), flip)
    v_rev = dot(flip, x.astype(BF), 1, 1).astype(BF)
    pad[0:16, :] = jnp.zeros((16, 256), F32)
    pad[272:288, :] = jnp.zeros((16, 256), F32)
    pad[16:272, :] = x
    for m0 in range(4):
        sh = pad[16 - 4 * m0:272 - 4 * m0, :].astype(BF)
        xl[:, 256 * m0:256 * m0 + 128] = sh[:, 128:256]
        xl[:, 256 * m0 + 128:256 * m0 + 256] = sh[:, 0:128]
    pad[16:272, :] = g_rev
    for m0 in range(4):
        sh = pad[16 + 4 * m0:272 + 4 * m0, :].astype(BF)
        il[:, 256 * m0:256 * m0 + 128] = sh[:, 128:256]
        il[:, 256 * m0 + 128:256 * m0 + 256] = sh[:, 0:128]
    pad[16:272, :] = g
    for m0 in range(4):
        ifw[:, 256 * m0:256 * m0 + 256] = pad[16 + 4 * m0:272 + 4 * m0, :].astype(BF)
    phi[:, 0:128] = jnp.zeros((128, 128), BF)
    plo[:, 0:128] = jnp.zeros((128, 128), BF)
    prev = jnp.zeros((128, 128), F32)
    for u in range(128):
        row = jnp.broadcast_to(f_ref[pl.ds(2 * u + p, 1), :], (128, 128))
        turned = pltpu.roll(row, 0, 1, stride=1, stride_axis=0)
        band = jnp.where(keep, turned, prev)
        high = band.astype(BF)
        phi[:, 128 * (u + 1):128 * (u + 2)] = high
        plo[:, 128 * (u + 1):128 * (u + 2)] = (band - high.astype(F32)).astype(BF)
        prev = turned
    y_acc[...] = jnp.zeros((256, 256), F32)
    v_acc[...] = jnp.zeros((256, 256), F32)
    carry = jnp.zeros((128, 128), F32)
    before = jnp.zeros((128, 128), F32)

    def write(u, first, second):
        total = jnp.sum(jnp.where(early, first, second), axis=0, keepdims=True)
        of_ref[pl.ds(2 * u + p, 1), :] = total * (1.0 / 256.0)

    for m1 in range(16):
        n = 256 - 16 * m1
        lhs = jnp.concatenate([xl[0:n, :], il[16 * m1:256, :]], axis=0)

        def slabs(ref):
            return jnp.concatenate(
                [ref[:, 128 * k + 1024 * m1:128 * k + 1024 * m1 + 256] for k in range(8)], axis=0
            )

        res = dot(lhs, slabs(phi)) + dot(lhs, slabs(plo))
        y_acc[16 * m1:256, :] += res[0:n]
        v_acc[0:n, :] += res[n:]
        depth = 256 if n > 128 else 128
        rhs = ifw[16 * m1:256, :]
        if depth > n:
            rhs = jnp.concatenate([rhs, jnp.zeros((depth - n, 1024), BF)], axis=0)
        outer = dot(v_rev[:, 0:depth], rhs)
        for t in range(8):
            w = outer[0:128, 128 * t:128 * t + 128]
            w = w + (carry if t == 0 else outer[128:256, 128 * t - 128:128 * t])
            turned = pltpu.roll(w, 1, 1, stride=1, stride_axis=0)
            if 8 * m1 + t >= 2:
                write(8 * m1 + t - 2, before, turned)
            before = turned
        carry = outer[128:256, 896:1024]
    turned = pltpu.roll(carry, 1, 1, stride=1, stride_axis=0)
    write(126, before, turned)
    write(127, turned, jnp.zeros((128, 128), F32))
    for h in range(2):
        o_ref[pl.ds(1024 * p + 512 * h, 256, stride=2), :] = y_acc[:, 128 * h:128 * h + 128]
        back = v_acc[:, 128 * (1 - h):128 * (1 - h) + 128]
        o_ref[pl.ds(1024 * p + 512 * h + 1, 256, stride=2), :] = jnp.take_along_axis(back, lane_rev, axis=1)


SIB_IN, IN, FILT, OUT, GRAD, SIB_OUT = 0, 2, 4, 5, 7, 8


def main_kernel(
    gate_ref, values_ref, filters_ref, grad_ref, out_ref, ofg_ref,
    wide, mine, swap_in, xb, r, fb, hf, o, og, b, parts, swap_out,
    pad, xl, il, ifw, y_acc, v_acc, phi, plo, ssem, rsem, lsem,
):
    ctx = lax.axis_index("ctx")
    ch = lax.axis_index("ch")
    core = lax.rem(ch, 2)
    zl = lax.div(ch, 2)
    sibling = (ctx, zl * 2 + 1 - core)
    hub = zl * 128 + ctx
    place = lax.rem(ctx, 2) * 128 + lax.div(ctx, 2) * 2 + zl

    barrier = pltpu.get_barrier_semaphore()
    pl.semaphore_signal(barrier, inc=1, device_id=sibling, device_id_type=MESH)
    every_chip(
        lambda h2, p2, c2, ch2: pl.semaphore_signal(barrier, inc=1, device_id=(c2, ch2), device_id_type=MESH)
    )

    inner = (grad_ref[...].astype(F32) * gate_ref[...].astype(F32)).astype(BF)
    for s, signal in enumerate((values_ref[...], inner)):
        wide[...] = signal.astype(F32).T
        for c2 in range(2):
            for p in range(2):
                for z2 in range(2):
                    mine[c2, pl.ds((p * 256 + z2 * 128) * 2 + s, 128, stride=2), :] = (
                        wide[pl.ds(512 * z2 + 256 * c2 + p, 128, stride=2), :]
                    )
    fb[...] = filters_ref[:, pl.ds(pl.multiple_of(ch * 256, 256), 256)].T

    pl.semaphore_wait(barrier, 256)

    def send(src, dst, k, to):
        copy = pltpu.make_async_remote_copy(src, dst, ssem.at[k], rsem.at[k], device_id=to, device_id_type=MESH)
        copy.start()
        return copy

    def local(src, dst, k):
        copy = pltpu.make_async_copy(src, dst, lsem.at[k])
        copy.start()
        return copy

    def rows(ref, start, size):
        return ref.at[pl.ds(pl.multiple_of(start, size), size)]

    def landed(ref, count, k):
        pltpu.make_async_copy(ref.at[pl.ds(0, count)], ref.at[pl.ds(0, count)], rsem.at[k]).wait()

    def left(ref, count, k):
        pltpu.make_async_copy(ref.at[pl.ds(0, count)], ref.at[pl.ds(0, count)], ssem.at[k]).wait()

    swaps = [
        send(mine.at[1 - core, pl.ds(512 * p, 512)], swap_in.at[pl.ds(512 * p, 512)], SIB_IN + p, sibling)
        for p in range(2)
    ]
    own_f = local(rows(fb, 2 * ctx, 2), rows(hf, 2 * ctx, 2), 0)
    every_row(lambda c2: send(rows(fb, 2 * c2, 2), rows(hf, 2 * ctx, 2), FILT, (c2, ch)))
    own_in = []
    for p in range(2):
        swaps[p].wait_recv()
        for s in range(2):
            kept = mine[core, pl.ds(512 * p + s, 256, stride=2), :]
            got = swap_in[pl.ds(512 * p + s, 256, stride=2), :]
            xb[pl.ds(1024 * p + s, 256, stride=4), :] = jnp.where(core == 0, kept, got)
            xb[pl.ds(1024 * p + 2 + s, 256, stride=4), :] = jnp.where(core == 0, got, kept)
        own_in.append(local(rows(xb, 1024 * p + 4 * hub, 4), rows(r, 1024 * p + 4 * place, 4), 1 + p))
        every_chip(
            lambda h2, p2, c2, ch2: send(
                rows(xb, 1024 * p + 4 * h2, 4), rows(r, 1024 * p + 4 * place, 4), IN + p, (c2, ch2)
            )
        )
    own_out = []
    for p in range(2):
        own_in[p].wait()
        landed(r, 1020, IN + p)
        if p == 0:
            own_f.wait()
            landed(hf, 254, FILT)
        products(p, r, hf, o, og, pad, xl, il, ifw, y_acc, v_acc, phi, plo)
        own_out.append(local(rows(o, 1024 * p + 4 * place, 4), rows(b, 1024 * p + 4 * hub, 4), 3 + p))
        every_chip(
            lambda h2, p2, c2, ch2: send(
                rows(o, 1024 * p + 4 * p2, 4), rows(b, 1024 * p + 4 * hub, 4), OUT + p, (c2, ch2)
            )
        )
    own_g = local(rows(og, 2 * ctx, 2), rows(ofg_ref, 2 * ctx, 2), 5)
    every_row(lambda c2: send(rows(og, 2 * c2, 2), rows(ofg_ref, 2 * ctx, 2), GRAD, (c2, ch)))
    swaps_out = []
    for p in range(2):
        own_out[p].wait()
        landed(b, 1020, OUT + p)
        for s in range(2):
            for c2 in range(2):
                parts[c2, pl.ds(512 * p + s, 256, stride=2), :] = b[pl.ds(1024 * p + 2 * c2 + s, 256, stride=4), :]
        swaps_out.append(
            send(parts.at[1 - core, pl.ds(512 * p, 512)], swap_out.at[pl.ds(512 * p, 512)], SIB_OUT + p, sibling)
        )
    for p in range(2):
        swaps_out[p].wait_recv()
        for s in range(2):
            for z2 in range(2):
                at = pl.ds(512 * p + 256 * z2 + s, 128, stride=2)
                kept = parts[core, at, :]
                got = swap_out[at, :]
                out_ref[pl.ds(1024 * s + 512 * z2 + p, 128, stride=2), :] = jnp.where(core == 0, kept, got)
                out_ref[pl.ds(1024 * s + 512 * z2 + 256 + p, 128, stride=2), :] = jnp.where(core == 0, got, kept)
    own_g.wait()
    landed(ofg_ref, 254, GRAD)
    for p in range(2):
        swaps[p].wait_send()
        swaps_out[p].wait_send()
        left(xb, 1020, IN + p)
        left(o, 1020, OUT + p)
    left(fb, 254, FILT)
    left(og, 254, GRAD)


def unpack_kernel(b_ref, f_ref, grad_ref, gate_grad_ref, value_grad_ref, filter_grad_ref):
    gate_grad_ref[...] = b_ref[0:1024, :].T * grad_ref[...].astype(F32)
    value_grad_ref[...] = b_ref[1024:2048, :].T
    filter_grad_ref[...] = f_ref[...].T


def per_device(gate_in, values, filters, out_grad):
    def buf(rows, lanes=128, dtype=F32):
        return pltpu.VMEM((rows, lanes), dtype)

    out, fg = pl.pallas_call(
        main_kernel,
        out_shape=(jax.ShapeDtypeStruct((2048, 128), F32), jax.ShapeDtypeStruct((256, 128), F32)),
        in_specs=[VM] * 4,
        out_specs=(VM, VM),
        scratch_shapes=[
            buf(1024), pltpu.VMEM((2, 1024, 128), F32), buf(1024), buf(2048), buf(2048), buf(256), buf(256),
            buf(2048), buf(256), buf(2048), pltpu.VMEM((2, 1024, 128), F32), buf(1024),
            buf(288, 256), buf(256, 1024, BF), buf(256, 1024, BF), buf(256, 1024, BF),
            buf(256, 256), buf(256, 256), buf(128, 16512, BF), buf(128, 16512, BF),
            pltpu.SemaphoreType.DMA((10,)), pltpu.SemaphoreType.DMA((10,)), pltpu.SemaphoreType.DMA((6,)),
        ],
        name="through_hubs",
        compiler_params=pltpu.CompilerParams(
            collective_id=0, has_side_effects=True, vmem_limit_bytes=48 * 1024 * 1024
        ),
    )(gate_in, values, filters, out_grad)
    return pl.pallas_call(
        unpack_kernel,
        out_shape=(
            jax.ShapeDtypeStruct((128, 1024), F32),
            jax.ShapeDtypeStruct((128, 1024), F32),
            jax.ShapeDtypeStruct((128, 256), F32),
        ),
        in_specs=[VM] * 3,
        out_specs=(VM,) * 3,
        name="unpack",
    )(out, fg, out_grad)


def solution(mesh):
    return jax.shard_map(
        per_device,
        mesh=mesh,
        in_specs=(P("ctx", "ch"), P("ctx", "ch"), P("ctx", None), P("ctx", "ch")),
        out_specs=(P("ctx", "ch"), P("ctx", "ch"), P("ctx", "ch")),
        check_vma=False,
    )
```

```python
import functools

import jax
import jax.numpy as jnp
from jax import lax
from jax.experimental import pallas as pl
from jax.experimental.pallas import tpu as pltpu
from jax.sharding import PartitionSpec as P

BF = jnp.bfloat16
F32 = jnp.float32
MESH = pl.DeviceIdType.MESH
VM = pl.BlockSpec(memory_space=pltpu.VMEM)


def dot(a, b, ca=1, cb=0):
    return lax.dot_general(a, b, (((ca,), (cb,)), ((), ())), preferred_element_type=F32)


def every_chip(visit):
    ctx = lax.axis_index("ctx")
    ch = lax.axis_index("ch")
    core = lax.rem(ch, 2)
    x = lax.rem(ctx, 4)
    y = lax.rem(lax.div(ctx, 4), 8)
    z = lax.div(ctx, 32) * 2 + lax.div(ch, 2)
    ys = [lax.rem(y + d, 8) * 4 for d in range(8)]
    zs = [lax.rem(z + d, 8) for d in range(8)]
    zls = [lax.rem(w, 2) for w in zs]
    zhs = [lax.div(w, 2) * 32 for w in zs]

    def body(i, _):
        x2 = lax.rem(x + i, 4)
        odd = lax.rem(x2, 2)
        shift = odd * 127
        for dz in range(8):
            for dy in range(8):
                def one(dz=dz, dy=dy):
                    ctx2 = zhs[dz] + ys[dy] + x2
                    visit(zls[dz] * 128 + ctx2, ctx2 + shift + zls[dz], ctx2, zls[dz] * 2 + core)
                if dz == 0 and dy == 0:
                    pl.when(i > 0)(one)
                else:
                    one()
        return 0

    lax.fori_loop(0, 4, body, 0)


def every_row(visit):
    ctx = lax.axis_index("ctx")

    def body(i, _):
        for k in range(8):
            def one(d=8 * i + k):
                visit(lax.rem(ctx + d, 128))
            if k == 0:
                pl.when(i > 0)(one)
            else:
                one()
        return 0

    lax.fori_loop(0, 16, body, 0)


def masks():
    row = lax.broadcasted_iota(jnp.int32, (128, 128), 0)
    lane = lax.broadcasted_iota(jnp.int32, (128, 128), 1)
    return row, lane


def flip_matrix():
    row = lax.broadcasted_iota(jnp.int32, (256, 256), 0)
    lane = lax.broadcasted_iota(jnp.int32, (256, 256), 1)
    return (row + lane == 255).astype(F32).astype(BF)


def bands(p, f_ref, phi, plo):
    row, lane = masks()
    keep = lane >= row
    phi[:, 0:128] = jnp.zeros((128, 128), BF)
    plo[:, 0:128] = jnp.zeros((128, 128), BF)
    prev = jnp.zeros((128, 128), F32)
    for u in range(128):
        taps = jnp.broadcast_to(f_ref[pl.ds(2 * u + p, 1), :], (128, 128))
        turned = pltpu.roll(taps, 0, 1, stride=1, stride_axis=0)
        band = jnp.where(keep, turned, prev)
        high = band.astype(BF)
        phi[:, 128 * (u + 1):128 * (u + 2)] = high
        plo[:, 128 * (u + 1):128 * (u + 2)] = (band - high.astype(F32)).astype(BF)
        prev = turned


def load_signal(p, s, r_ref):
    return jnp.concatenate(
        [r_ref[pl.ds(1024 * p + 512 * h + s, 256, stride=2), :] for h in range(2)], axis=1
    )


def convolve(p, r_ref, o_ref, pad, xl, il, y_acc, v_acc, phi, plo):
    pad[0:16, :] = jnp.zeros((16, 256), F32)
    pad[272:288, :] = jnp.zeros((16, 256), F32)
    pad[16:272, :] = load_signal(p, 0, r_ref)
    for m0 in range(4):
        sh = pad[16 - 4 * m0:272 - 4 * m0, :].astype(BF)
        xl[:, 256 * m0:256 * m0 + 128] = sh[:, 128:256]
        xl[:, 256 * m0 + 128:256 * m0 + 256] = sh[:, 0:128]
    pad[16:272, :] = dot(load_signal(p, 1, r_ref).astype(BF), flip_matrix())
    for m0 in range(4):
        sh = pad[16 + 4 * m0:272 + 4 * m0, :].astype(BF)
        il[:, 256 * m0:256 * m0 + 128] = sh[:, 128:256]
        il[:, 256 * m0 + 128:256 * m0 + 256] = sh[:, 0:128]
    y_acc[...] = jnp.zeros((256, 256), F32)
    v_acc[...] = jnp.zeros((256, 256), F32)
    for m1 in range(16):
        n = 256 - 16 * m1
        lhs = jnp.concatenate([xl[0:n, :], il[16 * m1:256, :]], axis=0)

        def slabs(ref):
            return jnp.concatenate(
                [ref[:, 128 * k + 1024 * m1:128 * k + 1024 * m1 + 256] for k in range(8)], axis=0
            )

        res = dot(lhs, slabs(phi)) + dot(lhs, slabs(plo))
        y_acc[16 * m1:256, :] += res[0:n]
        v_acc[0:n, :] += res[n:]
    lane_rev = 127 - lax.broadcasted_iota(jnp.int32, (256, 128), 1)
    for h in range(2):
        o_ref[pl.ds(1024 * p + 512 * h, 256, stride=2), :] = y_acc[:, 128 * h:128 * h + 128]
        back = v_acc[:, 128 * (1 - h):128 * (1 - h) + 128]
        o_ref[pl.ds(1024 * p + 512 * h + 1, 256, stride=2), :] = jnp.take_along_axis(back, lane_rev, axis=1)


def correlate(p, r_ref, of_ref, pad, ifw):
    row, lane = masks()
    early = lane <= row
    v_rev = dot(flip_matrix(), load_signal(p, 0, r_ref).astype(BF), 1, 1).astype(BF)
    pad[272:288, :] = jnp.zeros((16, 256), F32)
    pad[16:272, :] = load_signal(p, 1, r_ref)
    for m0 in range(4):
        ifw[:, 256 * m0:256 * m0 + 256] = pad[16 + 4 * m0:272 + 4 * m0, :].astype(BF)
    carry = jnp.zeros((128, 128), F32)
    before = jnp.zeros((128, 128), F32)

    def write(u, first, second):
        of_ref[pl.ds(2 * u + p, 1), :] = jnp.sum(jnp.where(early, first, second), axis=0, keepdims=True)

    for m1 in range(16):
        n = 256 - 16 * m1
        depth = 256 if n > 128 else 128
        rhs = ifw[16 * m1:256, :]
        if depth > n:
            rhs = jnp.concatenate([rhs, jnp.zeros((depth - n, 1024), BF)], axis=0)
        outer = dot(v_rev[:, 0:depth], rhs)
        for t in range(8):
            w = outer[0:128, 128 * t:128 * t + 128]
            w = w + (carry if t == 0 else outer[128:256, 128 * t - 128:128 * t])
            turned = pltpu.roll(w, 1, 1, stride=1, stride_axis=0)
            if 8 * m1 + t >= 2:
                write(8 * m1 + t - 2, before, turned)
            before = turned
        carry = outer[128:256, 896:1024]
    turned = pltpu.roll(carry, 1, 1, stride=1, stride_axis=0)
    write(126, before, turned)
    write(127, turned, jnp.zeros((128, 128), F32))


SIB_IN, IN, FILT, OUT, GRAD, SIB_OUT = 0, 2, 4, 5, 7, 8


def main_kernel(
    gate_ref, values_ref, filters_ref, grad_ref, gate_grad_ref, value_grad_ref, filter_grad_ref,
    gate_v, values_v, filters_v, grad_v,
    mine, swap_in, xb, r, fb, hf, o, og, b, fg, parts, swap_out,
    pad, xl, il, ifw, y_acc, v_acc, phi, plo, final, final_f, ssem, rsem, lsem,
):
    ctx = lax.axis_index("ctx")
    ch = lax.axis_index("ch")
    core = lax.rem(ch, 2)
    zl = lax.div(ch, 2)
    sibling = (ctx, zl * 2 + 1 - core)
    hub = zl * 128 + ctx
    place = lax.rem(ctx, 2) * 128 + lax.div(ctx, 2) * 2 + zl

    loads = [
        pltpu.make_async_copy(src, dst, lsem.at[6 + k])
        for k, (src, dst) in enumerate((
            (values_ref, values_v), (gate_ref, gate_v), (grad_ref, grad_v),
            (filters_ref.at[:, pl.ds(pl.multiple_of(ch * 256, 256), 256)], filters_v),
        ))
    ]
    for copy in loads:
        copy.start()
    barrier = pltpu.get_barrier_semaphore()
    pl.semaphore_signal(barrier, inc=1, device_id=sibling, device_id_type=MESH)
    every_chip(
        lambda h2, p2, c2, ch2: pl.semaphore_signal(barrier, inc=1, device_id=(c2, ch2), device_id_type=MESH)
    )
    for copy in loads:
        copy.wait()

    def pack(p):
        for z2 in range(2):
            for c2 in range(2):
                lanes = slice(512 * z2 + 256 * c2 + 128 * p, 512 * z2 + 256 * c2 + 128 * p + 128)
                inner = (grad_v[:, lanes].astype(F32) * gate_v[:, lanes].astype(F32)).astype(BF)
                for s, signal in enumerate((values_v[:, lanes], inner)):
                    mine[c2, pl.ds((p * 256 + z2 * 128) * 2 + s, 128, stride=2), :] = signal.astype(F32).T

    for p in range(2):
        fb[pl.ds(p, 128, stride=2), :] = filters_v[:, 128 * p:128 * p + 128].T
    pack(0)

    pl.semaphore_wait(barrier, 256)

    def send(src, dst, k, to):
        copy = pltpu.make_async_remote_copy(src, dst, ssem.at[k], rsem.at[k], device_id=to, device_id_type=MESH)
        copy.start()
        return copy

    def local(src, dst, k):
        copy = pltpu.make_async_copy(src, dst, lsem.at[k])
        copy.start()
        return copy

    def rows(ref, start, size):
        return ref.at[pl.ds(pl.multiple_of(start, size), size)]

    def landed(ref, count, k):
        pltpu.make_async_copy(ref.at[pl.ds(0, count)], ref.at[pl.ds(0, count)], rsem.at[k]).wait()

    def left(ref, count, k):
        pltpu.make_async_copy(ref.at[pl.ds(0, count)], ref.at[pl.ds(0, count)], ssem.at[k]).wait()

    def swap(p):
        return send(mine.at[1 - core, pl.ds(512 * p, 512)], swap_in.at[pl.ds(512 * p, 512)], SIB_IN + p, sibling)

    swaps = [swap(0)]
    own_f = local(rows(fb, 2 * ctx, 2), rows(hf, 2 * ctx, 2), 0)
    every_row(lambda c2: send(rows(fb, 2 * c2, 2), rows(hf, 2 * ctx, 2), FILT, (c2, ch)))
    pack(1)
    swaps.append(swap(1))
    own_in = []
    for p in range(2):
        swaps[p].wait_recv()
        for s in range(2):
            kept = mine[core, pl.ds(512 * p + s, 256, stride=2), :]
            got = swap_in[pl.ds(512 * p + s, 256, stride=2), :]
            xb[pl.ds(1024 * p + s, 256, stride=4), :] = jnp.where(core == 0, kept, got)
            xb[pl.ds(1024 * p + 2 + s, 256, stride=4), :] = jnp.where(core == 0, got, kept)
        own_in.append(local(rows(xb, 1024 * p + 4 * hub, 4), rows(r, 1024 * p + 4 * place, 4), 1 + p))
        every_chip(
            lambda h2, p2, c2, ch2: send(
                rows(xb, 1024 * p + 4 * h2, 4), rows(r, 1024 * p + 4 * place, 4), IN + p, (c2, ch2)
            )
        )
    own_f.wait()
    landed(hf, 254, FILT)
    for p in range(2):
        bands(p, hf, phi.at[p], plo.at[p])
    own_out = []
    for p in range(2):
        own_in[p].wait()
        landed(r, 1020, IN + p)
        convolve(p, r, o, pad, xl, il, y_acc, v_acc, phi.at[p], plo.at[p])
        own_out.append(local(rows(o, 1024 * p + 4 * place, 4), rows(b, 1024 * p + 4 * hub, 4), 3 + p))
        every_chip(
            lambda h2, p2, c2, ch2: send(
                rows(o, 1024 * p + 4 * p2, 4), rows(b, 1024 * p + 4 * hub, 4), OUT + p, (c2, ch2)
            )
        )
        correlate(p, r, og, pad, ifw)
    stores = []
    own_g = local(rows(og, 2 * ctx, 2), rows(fg, 2 * ctx, 2), 5)
    every_row(lambda c2: send(rows(og, 2 * c2, 2), rows(fg, 2 * ctx, 2), GRAD, (c2, ch)))
    for p in range(2):
        own_out[p].wait()
        landed(b, 1020, OUT + p)
        for s in range(2):
            for c2 in range(2):
                parts[c2, pl.ds(512 * p + s, 256, stride=2), :] = b[pl.ds(1024 * p + 2 * c2 + s, 256, stride=4), :]
        back = send(parts.at[1 - core, pl.ds(512 * p, 512)], swap_out.at[pl.ds(512 * p, 512)], SIB_OUT + p, sibling)
        back.wait_recv()
        for z2 in range(2):
            for s in range(2):
                at = pl.ds(512 * p + 256 * z2 + s, 128, stride=2)
                kept = parts[core, at, :]
                got = swap_out[at, :]
                lane = 512 * z2 + 128 * p
                first = jnp.where(core == 0, kept, got).T
                second = jnp.where(core == 0, got, kept).T
                if s == 0:
                    first = first * grad_v[:, lane:lane + 128].astype(F32)
                    second = second * grad_v[:, lane + 256:lane + 384].astype(F32)
                final[s, :, lane:lane + 128] = first
                final[s, :, lane + 256:lane + 384] = second
                for c2 in range(2):
                    lanes = pl.ds(lane + 256 * c2, 128)
                    stores.append(local(final.at[s, :, lanes], (gate_grad_ref, value_grad_ref)[s].at[:, lanes], 10 + len(stores)))
        back.wait_send()
    own_g.wait()
    landed(fg, 254, GRAD)
    for p in range(2):
        final_f[:, 128 * p:128 * p + 128] = fg[pl.ds(p, 128, stride=2), :].T * (1.0 / 256.0)
    stores.append(local(final_f, filter_grad_ref, 10 + len(stores)))
    for p in range(2):
        swaps[p].wait_send()
        left(xb, 1020, IN + p)
        left(o, 1020, OUT + p)
    left(fb, 254, FILT)
    left(og, 254, GRAD)
    for copy in stores:
        copy.wait()


def hand_over_kernel(a_ref, b_ref, c_ref, oa_ref, ob_ref, oc_ref, sem):
    copies = [
        pltpu.make_async_copy(src, dst, sem.at[k])
        for k, (src, dst) in enumerate(((a_ref, oa_ref), (b_ref, ob_ref), (c_ref, oc_ref)))
    ]
    for copy in copies:
        copy.start()
    for copy in copies:
        copy.wait()


def per_device(gate_in, values, filters, out_grad):
    def buf(rows, lanes=128, dtype=F32):
        return pltpu.VMEM((rows, lanes), dtype)

    anywhere = pl.BlockSpec(memory_space=pltpu.HBM)
    shapes = (
        jax.ShapeDtypeStruct((128, 1024), F32),
        jax.ShapeDtypeStruct((128, 1024), F32),
        jax.ShapeDtypeStruct((128, 256), F32),
    )
    results = pl.pallas_call(
        main_kernel,
        out_shape=shapes,
        in_specs=[anywhere] * 4,
        out_specs=(anywhere,) * 3,
        scratch_shapes=[
            buf(128, 1024, BF), buf(128, 1024, BF), buf(128, 256), buf(128, 1024, BF),
            pltpu.VMEM((2, 1024, 128), F32), buf(1024), buf(2048), buf(2048), buf(256), buf(256),
            buf(2048), buf(256), buf(2048), buf(256), pltpu.VMEM((2, 1024, 128), F32), buf(1024),
            buf(288, 256), buf(256, 1024, BF), buf(256, 1024, BF), buf(256, 1024, BF),
            buf(256, 256), buf(256, 256), pltpu.VMEM((2, 128, 16512), BF), pltpu.VMEM((2, 128, 16512), BF),
            pltpu.VMEM((2, 128, 1024), F32), buf(128, 256),
            pltpu.SemaphoreType.DMA((10,)), pltpu.SemaphoreType.DMA((10,)), pltpu.SemaphoreType.DMA((27,)),
        ],
        name="through_hubs",
        compiler_params=pltpu.CompilerParams(
            collective_id=0, has_side_effects=True, vmem_limit_bytes=62 * 1024 * 1024
        ),
    )(gate_in, values, filters, out_grad)
    return pl.pallas_call(
        hand_over_kernel,
        out_shape=shapes,
        in_specs=[anywhere] * 3,
        out_specs=(anywhere,) * 3,
        scratch_shapes=[pltpu.SemaphoreType.DMA((3,))],
        name="hand_over",
        compiler_params=pltpu.CompilerParams(vmem_limit_bytes=62 * 1024 * 1024),
    )(*results)


def solution(mesh):
    return jax.shard_map(
        per_device,
        mesh=mesh,
        in_specs=(P("ctx", "ch"), P("ctx", "ch"), P("ctx", None), P("ctx", "ch")),
        out_specs=(P("ctx", "ch"), P("ctx", "ch"), P("ctx", "ch")),
        check_vma=False,
    )
```

```python
import functools

import jax
import jax.numpy as jnp
from jax import lax
from jax.experimental import pallas as pl
from jax.experimental.pallas import tpu as pltpu
from jax.sharding import PartitionSpec as P

BF = jnp.bfloat16
F32 = jnp.float32
MESH = pl.DeviceIdType.MESH
VM = pl.BlockSpec(memory_space=pltpu.VMEM)


def dot(a, b, ca=1, cb=0):
    return lax.dot_general(a, b, (((ca,), (cb,)), ((), ())), preferred_element_type=F32)


def every_chip(visit):
    ctx = lax.axis_index("ctx")
    ch = lax.axis_index("ch")
    core = lax.rem(ch, 2)
    x = lax.rem(ctx, 4)
    y = lax.rem(lax.div(ctx, 4), 8)
    z = lax.div(ctx, 32) * 2 + lax.div(ch, 2)
    ys = [lax.rem(y + d, 8) * 4 for d in range(8)]
    zs = [lax.rem(z + d, 8) for d in range(8)]
    zls = [lax.rem(w, 2) for w in zs]
    zhs = [lax.div(w, 2) * 32 for w in zs]

    def body(i, _):
        x2 = lax.rem(x + i, 4)
        odd = lax.rem(x2, 2)
        shift = odd * 127
        for dz in range(8):
            for dy in range(8):
                def one(dz=dz, dy=dy):
                    ctx2 = zhs[dz] + ys[dy] + x2
                    visit(zls[dz] * 128 + ctx2, ctx2 + shift + zls[dz], ctx2, zls[dz] * 2 + core)
                if dz == 0 and dy == 0:
                    pl.when(i > 0)(one)
                else:
                    one()
        return 0

    lax.fori_loop(0, 4, body, 0)


def every_row(visit):
    ctx = lax.axis_index("ctx")

    def body(i, _):
        for k in range(8):
            def one(d=8 * i + k):
                visit(lax.rem(ctx + d, 128))
            if k == 0:
                pl.when(i > 0)(one)
            else:
                one()
        return 0

    lax.fori_loop(0, 16, body, 0)


def products(p, r_ref, f_ref, o_ref, of_ref, pad, xl, il, ifw, y_acc, v_acc, phi, plo):
    ri = lax.broadcasted_iota(jnp.int32, (256, 256), 0)
    ci = lax.broadcasted_iota(jnp.int32, (256, 256), 1)
    flip = (ri + ci == 255).astype(F32).astype(BF)
    row128 = lax.broadcasted_iota(jnp.int32, (128, 128), 0)
    lane128 = lax.broadcasted_iota(jnp.int32, (128, 128), 1)
    keep = lane128 >= row128
    early = lane128 <= row128
    lane_rev = 127 - lax.broadcasted_iota(jnp.int32, (256, 128), 1)

    def load(s):
        return jnp.concatenate(
            [r_ref[pl.ds(1024 * p + 512 * h + s, 256, stride=2), :] for h in range(2)], axis=1
        )

    x = load(0)
    g = load(1)
    g_rev = dot(g.astype(BF), flip)
    v_rev = dot(flip, x.astype(BF), 1, 1).astype(BF)
    pad[0:16, :] = jnp.zeros((16, 256), F32)
    pad[272:288, :] = jnp.zeros((16, 256), F32)
    pad[16:272, :] = x
    for m0 in range(4):
        sh = pad[16 - 4 * m0:272 - 4 * m0, :].astype(BF)
        xl[:, 256 * m0:256 * m0 + 128] = sh[:, 128:256]
        xl[:, 256 * m0 + 128:256 * m0 + 256] = sh[:, 0:128]
    pad[16:272, :] = g_rev
    for m0 in range(4):
        sh = pad[16 + 4 * m0:272 + 4 * m0, :].astype(BF)
        il[:, 256 * m0:256 * m0 + 128] = sh[:, 128:256]
        il[:, 256 * m0 + 128:256 * m0 + 256] = sh[:, 0:128]
    pad[16:272, :] = g
    for m0 in range(4):
        ifw[:, 256 * m0:256 * m0 + 256] = pad[16 + 4 * m0:272 + 4 * m0, :].astype(BF)
    phi[:, 0:128] = jnp.zeros((128, 128), BF)
    plo[:, 0:128] = jnp.zeros((128, 128), BF)
    prev = jnp.zeros((128, 128), F32)
    for u in range(128):
        row = jnp.broadcast_to(f_ref[pl.ds(2 * u + p, 1), :], (128, 128))
        turned = pltpu.roll(row, 0, 1, stride=1, stride_axis=0)
        band = jnp.where(keep, turned, prev)
        high = band.astype(BF)
        phi[:, 128 * (u + 1):128 * (u + 2)] = high
        plo[:, 128 * (u + 1):128 * (u + 2)] = (band - high.astype(F32)).astype(BF)
        prev = turned
    y_acc[...] = jnp.zeros((256, 256), F32)
    v_acc[...] = jnp.zeros((256, 256), F32)
    carry = jnp.zeros((128, 128), F32)
    before = jnp.zeros((128, 128), F32)

    def write(u, first, second):
        total = jnp.sum(jnp.where(early, first, second), axis=0, keepdims=True)
        of_ref[pl.ds(2 * u + p, 1), :] = total

    for m1 in range(16):
        n = 256 - 16 * m1
        lhs = jnp.concatenate([xl[0:n, :], il[16 * m1:256, :]], axis=0)

        def slabs(ref):
            return jnp.concatenate(
                [ref[:, 128 * k + 1024 * m1:128 * k + 1024 * m1 + 256] for k in range(8)], axis=0
            )

        res = dot(lhs, slabs(phi)) + dot(lhs, slabs(plo))
        y_acc[16 * m1:256, :] += res[0:n]
        v_acc[0:n, :] += res[n:]
        depth = 256 if n > 128 else 128
        rhs = ifw[16 * m1:256, :]
        if depth > n:
            rhs = jnp.concatenate([rhs, jnp.zeros((depth - n, 1024), BF)], axis=0)
        outer = dot(v_rev[:, 0:depth], rhs)
        for t in range(8):
            w = outer[0:128, 128 * t:128 * t + 128]
            w = w + (carry if t == 0 else outer[128:256, 128 * t - 128:128 * t])
            turned = pltpu.roll(w, 1, 1, stride=1, stride_axis=0)
            if 8 * m1 + t >= 2:
                write(8 * m1 + t - 2, before, turned)
            before = turned
        carry = outer[128:256, 896:1024]
    turned = pltpu.roll(carry, 1, 1, stride=1, stride_axis=0)
    write(126, before, turned)
    write(127, turned, jnp.zeros((128, 128), F32))
    for h in range(2):
        o_ref[pl.ds(1024 * p + 512 * h, 256, stride=2), :] = y_acc[:, 128 * h:128 * h + 128]
        back = v_acc[:, 128 * (1 - h):128 * (1 - h) + 128]
        o_ref[pl.ds(1024 * p + 512 * h + 1, 256, stride=2), :] = jnp.take_along_axis(back, lane_rev, axis=1)


SIB_IN, IN, FILT, OUT, GRAD, SIB_OUT = 0, 2, 4, 5, 7, 8


def main_kernel(
    gate_ref, values_ref, filters_ref, grad_ref, conv_ref, back_ref, fgrad_ref,
    gate_v, values_v, filters_v, grad_v,
    mine, swap_in, xb, r, fb, hf, o, og, b, fg, parts, swap_out,
    pad, xl, il, ifw, y_acc, v_acc, phi, plo, ssem, rsem, lsem,
):
    ctx = lax.axis_index("ctx")
    ch = lax.axis_index("ch")
    core = lax.rem(ch, 2)
    zl = lax.div(ch, 2)
    sibling = (ctx, zl * 2 + 1 - core)
    hub = zl * 128 + ctx
    place = lax.rem(ctx, 2) * 128 + lax.div(ctx, 2) * 2 + zl

    loads = [
        pltpu.make_async_copy(src, dst, lsem.at[6 + k])
        for k, (src, dst) in enumerate((
            (values_ref, values_v), (gate_ref, gate_v), (grad_ref, grad_v),
            (filters_ref.at[:, pl.ds(pl.multiple_of(ch * 256, 256), 256)], filters_v),
        ))
    ]
    for copy in loads:
        copy.start()
    barrier = pltpu.get_barrier_semaphore()
    pl.semaphore_signal(barrier, inc=1, device_id=sibling, device_id_type=MESH)
    every_chip(
        lambda h2, p2, c2, ch2: pl.semaphore_signal(barrier, inc=1, device_id=(c2, ch2), device_id_type=MESH)
    )
    for copy in loads:
        copy.wait()

    def pack(p):
        for z2 in range(2):
            for c2 in range(2):
                lanes = slice(512 * z2 + 256 * c2 + 128 * p, 512 * z2 + 256 * c2 + 128 * p + 128)
                inner = (grad_v[:, lanes].astype(F32) * gate_v[:, lanes].astype(F32)).astype(BF)
                for s, signal in enumerate((values_v[:, lanes], inner)):
                    mine[c2, pl.ds((p * 256 + z2 * 128) * 2 + s, 128, stride=2), :] = signal.astype(F32).T

    for p in range(2):
        fb[pl.ds(p, 128, stride=2), :] = filters_v[:, 128 * p:128 * p + 128].T
    pack(0)

    pl.semaphore_wait(barrier, 256)

    def send(src, dst, k, to):
        copy = pltpu.make_async_remote_copy(src, dst, ssem.at[k], rsem.at[k], device_id=to, device_id_type=MESH)
        copy.start()
        return copy

    def local(src, dst, k):
        copy = pltpu.make_async_copy(src, dst, lsem.at[k])
        copy.start()
        return copy

    def rows(ref, start, size):
        return ref.at[pl.ds(pl.multiple_of(start, size), size)]

    def landed(ref, count, k):
        pltpu.make_async_copy(ref.at[pl.ds(0, count)], ref.at[pl.ds(0, count)], rsem.at[k]).wait()

    def left(ref, count, k):
        pltpu.make_async_copy(ref.at[pl.ds(0, count)], ref.at[pl.ds(0, count)], ssem.at[k]).wait()

    def swap(p):
        return send(mine.at[1 - core, pl.ds(512 * p, 512)], swap_in.at[pl.ds(512 * p, 512)], SIB_IN + p, sibling)

    swaps = [swap(0)]
    own_f = local(rows(fb, 2 * ctx, 2), rows(hf, 2 * ctx, 2), 0)
    every_row(lambda c2: send(rows(fb, 2 * c2, 2), rows(hf, 2 * ctx, 2), FILT, (c2, ch)))
    pack(1)
    swaps.append(swap(1))
    own_in = []
    for p in range(2):
        swaps[p].wait_recv()
        for s in range(2):
            kept = mine[core, pl.ds(512 * p + s, 256, stride=2), :]
            got = swap_in[pl.ds(512 * p + s, 256, stride=2), :]
            xb[pl.ds(1024 * p + s, 256, stride=4), :] = jnp.where(core == 0, kept, got)
            xb[pl.ds(1024 * p + 2 + s, 256, stride=4), :] = jnp.where(core == 0, got, kept)
        own_in.append(local(rows(xb, 1024 * p + 4 * hub, 4), rows(r, 1024 * p + 4 * place, 4), 1 + p))
        every_chip(
            lambda h2, p2, c2, ch2: send(
                rows(xb, 1024 * p + 4 * h2, 4), rows(r, 1024 * p + 4 * place, 4), IN + p, (c2, ch2)
            )
        )
    own_out = []
    for p in range(2):
        own_in[p].wait()
        landed(r, 1020, IN + p)
        if p == 0:
            own_f.wait()
            landed(hf, 254, FILT)
        products(p, r, hf, o, og, pad, xl, il, ifw, y_acc, v_acc, phi, plo)
        own_out.append(local(rows(o, 1024 * p + 4 * place, 4), rows(b, 1024 * p + 4 * hub, 4), 3 + p))
        every_chip(
            lambda h2, p2, c2, ch2: send(
                rows(o, 1024 * p + 4 * p2, 4), rows(b, 1024 * p + 4 * hub, 4), OUT + p, (c2, ch2)
            )
        )
    own_g = local(rows(og, 2 * ctx, 2), rows(fg, 2 * ctx, 2), 5)
    every_row(lambda c2: send(rows(og, 2 * c2, 2), rows(fg, 2 * ctx, 2), GRAD, (c2, ch)))
    for p in range(2):
        own_out[p].wait()
        landed(b, 1020, OUT + p)
        for s in range(2):
            for c2 in range(2):
                parts[c2, pl.ds(512 * p + s, 256, stride=2), :] = b[pl.ds(1024 * p + 2 * c2 + s, 256, stride=4), :]
        back = send(parts.at[1 - core, pl.ds(512 * p, 512)], swap_out.at[pl.ds(512 * p, 512)], SIB_OUT + p, sibling)
        back.wait_recv()
        for s, out in enumerate((conv_ref, back_ref)):
            for z2 in range(2):
                at = pl.ds(512 * p + 256 * z2 + s, 128, stride=2)
                kept = parts[core, at, :]
                got = swap_out[at, :]
                lane = 512 * z2 + 128 * p
                out[:, lane:lane + 128] = jnp.where(core == 0, kept, got).T
                out[:, lane + 256:lane + 384] = jnp.where(core == 0, got, kept).T
        back.wait_send()
    own_g.wait()
    landed(fg, 254, GRAD)
    for p in range(2):
        fgrad_ref[:, 128 * p:128 * p + 128] = fg[pl.ds(p, 128, stride=2), :].T
    for p in range(2):
        swaps[p].wait_send()
        left(xb, 1020, IN + p)
        left(o, 1020, OUT + p)
    left(fb, 254, FILT)
    left(og, 254, GRAD)


def per_device(gate_in, values, filters, out_grad):
    def buf(rows, lanes=128, dtype=F32):
        return pltpu.VMEM((rows, lanes), dtype)

    anywhere = pl.BlockSpec(memory_space=pltpu.HBM)
    conv, back, fg = pl.pallas_call(
        main_kernel,
        out_shape=(
            jax.ShapeDtypeStruct((128, 1024), F32),
            jax.ShapeDtypeStruct((128, 1024), F32),
            jax.ShapeDtypeStruct((128, 256), F32),
        ),
        in_specs=[anywhere] * 4,
        out_specs=(VM,) * 3,
        scratch_shapes=[
            buf(128, 1024, BF), buf(128, 1024, BF), buf(128, 256), buf(128, 1024, BF),
            pltpu.VMEM((2, 1024, 128), F32), buf(1024), buf(2048), buf(2048), buf(256), buf(256),
            buf(2048), buf(256), buf(2048), buf(256), pltpu.VMEM((2, 1024, 128), F32), buf(1024),
            buf(288, 256), buf(256, 1024, BF), buf(256, 1024, BF), buf(256, 1024, BF),
            buf(256, 256), buf(256, 256), buf(128, 16512, BF), buf(128, 16512, BF),
            pltpu.SemaphoreType.DMA((10,)), pltpu.SemaphoreType.DMA((10,)), pltpu.SemaphoreType.DMA((10,)),
        ],
        name="through_hubs",
        compiler_params=pltpu.CompilerParams(
            collective_id=0, has_side_effects=True, vmem_limit_bytes=62 * 1024 * 1024
        ),
    )(gate_in, values, filters, out_grad)
    return out_grad.astype(F32) * conv, back, fg * (1.0 / 256.0)


def solution(mesh):
    return jax.shard_map(
        per_device,
        mesh=mesh,
        in_specs=(P("ctx", "ch"), P("ctx", "ch"), P("ctx", None), P("ctx", "ch")),
        out_specs=(P("ctx", "ch"), P("ctx", "ch"), P("ctx", "ch")),
        check_vma=False,
    )
```
